128 devices in a mesh: tasks: 32 (over y, x, core), grp: 4 (over z).
Axes of the slice: x: 4, y: 4, z: 4, core: 2. Of those that a mesh axis runs over, the one named last changes fastest.
Arguments:
- t2_store: bfloat16 [4, 2048, 128, 128], P('grp', 'tasks'), may hold values from -0.046875 to 0.046875
- ovvo_store: bfloat16 [4096, 128, 128], P(('tasks', 'grp')), may hold values from -6 to 6
- ovvv_store: bfloat16 [4096, 128, 128], P(('tasks', 'grp')), may hold values from -6 to 6
- dressing: bfloat16 [128, 128], replicated, may hold values from -0.5 to 0.5
- t_home: int32 [4, 2048], P('grp'), may hold values from 0 to 2047, as said below
- t_send: int32 [4, 32, 32, 2], P('grp', 'tasks'), may hold values from 0 to 2047, as said below
- w_home: int32 [4096], replicated, may hold values from 0 to 4095, as said below
- w_send: int32 [128, 128, 1], P(('tasks', 'grp')), may hold values from 0 to 4095, as said below
- task_t: int32 [4, 32, 32, 32], P('grp', 'tasks'), may hold values from 0 to 63
- task_w: int32 [4, 32, 32, 32], P('grp', 'tasks'), may hold values from 0 to 127
- recv_rows: int32 [4, 32, 32, 1], P('grp', 'tasks'), may hold values from 0 to 15, as said below
- pair_orbitals: int32 [32, 2], replicated, may hold values from 0 to 299
- eps_occ: float32 [300], replicated, may hold values from -0.9 to -0.4
- eps_vir: float32 [1024], replicated, may hold values from 0.3 to 1.2
Outputs:
- amplitude_update: float32 [4, 512, 128, 128], P('grp', 'tasks')
The draws below stay inside these ranges and needn't reach their ends.
Inputs may be any that keep to these rules, and one draw needn't show every extreme that they name: Each row t_home[g] is a permutation; tile id n of group g lies in storage row t_home[g, n], on device t_home[g, n] // 64 of tasks. t_send[g, o, d, c] is a tile id stored on owner o: t_home[g, t_send[g, o, d, c]] // 64 equals o. w_home is a permutation; tile id n lies in storage row w_home[n], on the device with index w_home[n] // 32 = tasks index * 4 + grp index. w_send[o, q, c] is a tile id stored on device o: w_home[w_send[o, q, c]] // 32 equals o. For each g and o, every value below 16 appears exactly twice among recv_rows[g, o].
All inputs are finite; a program needn't handle non-finite values.
Results may differ from the reference program's by a relative error of at most 0.0029.
Values may be sent and summed in bfloat16 or wider, within the bound.
No kernel may reach another device: no remote copies, remote signals or barrier semaphores. Data moves between devices by JAX's collectives and lax.ppermute only.
A program may use at most 64 MiB of HBM per device.

```python
from functools import partial
import jax
import jax.numpy as jnp
from jax import lax

TILE = 128
VIRT = 1024
NOCC = 300
T_DEV = 64
W_DEV = 32
CAP_T = 2
CAP_W = 1
TPS = 32
R_DEV = 16
NV = 8
CAP_R = 1
FR = 32
FT = 64
OWNERS = 128
FW = 128
T_TILES = 2048
W_TILES = 4096
PAIRS = 32
N_TASKS = 32
N_GRP = 4


def shuffled(total, seed_key):
    return jax.random.permutation(seed_key, total)


def tile_layout(key, tables, total, per_owner, owners, dests, capacity):
    home_key, row_key = jax.random.split(jax.random.fold_in(key, 101))
    seed_keys = jax.random.split(home_key, tables)
    home_rows = jax.vmap(partial(shuffled, total))(seed_keys).astype(jnp.int32)
    inverse = jnp.argsort(home_rows, axis=1).astype(jnp.int32)
    local_rows = jax.random.randint(row_key, (tables, owners, dests, capacity), 0, per_owner).astype(jnp.int32)
    owner_grid = jnp.arange(owners, dtype=jnp.int32)[None, :, None, None]
    dest_grid = jnp.arange(dests, dtype=jnp.int32)[None, None, :, None]
    slot_grid = jnp.arange(capacity, dtype=jnp.int32)[None, None, None, :]
    position = owner_grid * per_owner + local_rows
    first_pos = home_rows[:, 0]
    first_owner = first_pos // per_owner
    first_mask = (owner_grid == first_owner[:, None, None, None]) & (dest_grid == 0) & (slot_grid == 0)
    position = jnp.where(first_mask, first_pos[:, None, None, None], position)
    last_pos = home_rows[:, total - 1]
    last_owner = last_pos // per_owner
    last_mask = (owner_grid == last_owner[:, None, None, None]) & (dest_grid == dests - 1) & (slot_grid == capacity - 1)
    position = jnp.where(last_mask, last_pos[:, None, None, None], position)
    tile_ids = jnp.take_along_axis(inverse, position.reshape(tables, -1), axis=1)
    return (home_rows, tile_ids.reshape(tables, owners, dests, capacity).astype(jnp.int32))


def draw_t_home(key, part):
    home_rows, tile_ids = tile_layout(key, N_GRP, T_TILES, T_DEV, N_TASKS, N_TASKS, CAP_T)
    return home_rows


def draw_t_send(key, part):
    home_rows, tile_ids = tile_layout(key, N_GRP, T_TILES, T_DEV, N_TASKS, N_TASKS, CAP_T)
    return tile_ids


def draw_w_home(key, part):
    home_rows, tile_ids = tile_layout(key, 1, W_TILES, W_DEV, OWNERS, OWNERS, CAP_W)
    return home_rows[0]


def draw_w_send(key, part):
    home_rows, tile_ids = tile_layout(key, 1, W_TILES, W_DEV, OWNERS, OWNERS, CAP_W)
    return tile_ids[0]


def draw_recv_rows(key, part):
    key = jax.random.fold_in(key, 7)
    seed_keys = jax.random.split(key, N_GRP * N_TASKS)
    orders = jax.vmap(partial(shuffled, 2 * R_DEV))(seed_keys).astype(jnp.int32)
    return (orders % R_DEV).astype(jnp.int32).reshape(N_GRP, N_TASKS, N_TASKS, CAP_R)


def place_ends(array, rng, smallest, high):
    dims = array.shape
    spot = [jax.random.randint(jax.random.fold_in(rng, axis), (), 0, dims[axis]) for axis in range(len(dims))]
    array = array.at[tuple(spot)].set(smallest)
    longest = dims.index(max(dims))
    spot[longest] = (spot[longest] + 1) % dims[longest]
    return array.at[tuple(spot)].set(high)


def shard_levels(stream_key, dims, pieces, smallest, top_value):
    def one(dim, blocks):
        heights = jax.random.uniform(jax.random.fold_in(jax.random.fold_in(stream_key, 6), dim), (blocks,), jnp.float32, smallest / len(pieces), top_value / len(pieces))
        return jnp.repeat(jnp.exp(heights), dims[dim] // blocks).reshape((-1,) + (1,) * (len(dims) - dim - 1))

    factor_of = one(*pieces[0])
    for cut in pieces[1:]:
        factor_of = factor_of * one(*cut)
    return factor_of


def bell_draw(rng, extent, spread, most, pieces=(), held_as=jnp.bfloat16):
    factor_of = shard_levels(rng, extent, pieces, -0.22, 0.18) if pieces else 1.0
    drawn = jax.random.normal(rng, extent, jnp.float32) * spread * factor_of
    return jnp.minimum(jnp.maximum(drawn, -most), most).astype(held_as)


def setup_inputs(seed: int = 0) -> dict:
    key_of = jax.random.split(jax.random.key(seed), 15)
    t2_store = bell_draw(key_of[0], (N_GRP, T_TILES, TILE, TILE), (4 * TILE * TPS) ** -0.5, 0.046875, ((0, 4), (1, 32)))
    ovvo_store = bell_draw(key_of[1], (W_TILES, TILE, TILE), 1.0, 6.0, ((0, 128),))
    ovvv_store = bell_draw(key_of[2], (W_TILES, TILE, TILE), 1.0, 6.0, ((0, 128),))
    dressing = bell_draw(key_of[3], (TILE, TILE), TILE ** -0.5, 0.5)
    t_home = draw_t_home(jax.random.fold_in(key_of[14], 71), 0)
    t_send = draw_t_send(jax.random.fold_in(key_of[14], 71), 0)
    w_home = draw_w_home(jax.random.fold_in(key_of[14], 71), 0)
    w_send = draw_w_send(jax.random.fold_in(key_of[14], 71), 0)
    task_t = place_ends(jax.random.randint(key_of[8], (N_GRP, N_TASKS, FR, TPS), 0, FT), jax.random.fold_in(key_of[8], 1), 0, FT - 1).astype(jnp.int32)
    task_w = place_ends(jax.random.randint(key_of[9], (N_GRP, N_TASKS, FR, TPS), 0, FW), jax.random.fold_in(key_of[9], 1), 0, FW - 1).astype(jnp.int32)
    recv_rows = draw_recv_rows(jax.random.fold_in(key_of[14], 71), 0)
    pair_orbitals = place_ends(jax.random.randint(key_of[11], (PAIRS, 2), 0, NOCC), jax.random.fold_in(key_of[11], 1), 0, NOCC - 1).astype(jnp.int32)
    eps_occ = jnp.clip(jax.random.uniform(key_of[12], (NOCC,), jnp.float32, -0.9, -0.4), -0.9, -0.4)
    eps_vir = jnp.clip(jax.random.uniform(key_of[13], (VIRT,), jnp.float32, 0.3, 1.2), 0.3, 1.2)
    return {"t2_store": t2_store, "ovvo_store": ovvo_store, "ovvv_store": ovvv_store, "dressing": dressing, "t_home": t_home, "t_send": t_send, "w_home": w_home, "w_send": w_send, "task_t": task_t, "task_w": task_w, "recv_rows": recv_rows, "pair_orbitals": pair_orbitals, "eps_occ": eps_occ, "eps_vir": eps_vir}


def segment_total(values, segment_ids):
    return jax.ops.segment_sum(values, segment_ids, num_segments=N_TASKS * R_DEV)


def reference(t2_store, ovvo_store, ovvv_store, dressing, t_home, t_send, w_home, w_send, task_t, task_w, recv_rows, pair_orbitals, eps_occ, eps_vir):
    tile_width = TILE
    groups = N_GRP
    workers = N_TASKS
    dressed = jnp.einsum("wab,bc->wac", ovvv_store.astype(jnp.float32), dressing.astype(jnp.float32))
    formed = (ovvo_store.astype(jnp.float32) + dressed).astype(jnp.bfloat16)

    def device_partials(position):
        group_pos = position // workers
        worker = position % workers
        t_ids = t_send[group_pos, :, worker, :].reshape(-1)
        t_fetched = t2_store[group_pos][t_home[group_pos][t_ids]]
        w_ids = w_send[:, worker * groups + group_pos, :].reshape(-1)
        w_fetched = formed[w_home[w_ids]]
        t_blocks = task_t[group_pos, worker].reshape(FR // 4, 4, TPS)
        w_blocks = task_w[group_pos, worker].reshape(FR // 4, 4, TPS)

        def product(indices):
            left_tiles = t_fetched[indices[0]].astype(jnp.float32)
            right_tiles = w_fetched[indices[1]].astype(jnp.float32)
            return jnp.einsum("skab,skbc->sac", left_tiles, right_tiles)

        block_sums = lax.map(product, (t_blocks, w_blocks))
        return block_sums.reshape(FR, tile_width, tile_width)

    partials = lax.map(device_partials, jnp.arange(groups * workers, dtype=jnp.int32))
    partials = partials.reshape(groups, workers * FR, tile_width, tile_width)
    offsets = jnp.arange(workers, dtype=jnp.int32) * R_DEV
    targets = jnp.transpose(recv_rows, (0, 2, 1, 3)) + offsets[None, None, :, None]
    targets = targets.reshape(groups, workers * FR).astype(jnp.int32)
    residual = jax.vmap(segment_total)(partials, targets)

    per_pair = NV * NV
    tile_ids = jnp.arange(workers * R_DEV, dtype=jnp.int32)
    group_ids = jnp.arange(groups, dtype=jnp.int32)
    pair_index = group_ids[:, None] * (PAIRS // groups) + tile_ids[None, :] // per_pair
    occupied = pair_orbitals[pair_index]
    occ_sum = eps_occ[occupied[..., 0]] + eps_occ[occupied[..., 1]]
    vir_tiles = eps_vir.reshape(NV, tile_width)
    left_vir = vir_tiles[(tile_ids // NV) % NV]
    right_vir = vir_tiles[tile_ids % NV]
    denominator = occ_sum[:, :, None, None] - left_vir[None, :, :, None] - right_vir[None, :, None, :]
    return residual / denominator
```

```python
import jax
import jax.numpy as jnp
from jax import lax
from jax.experimental import pallas as pl
from jax.experimental.pallas import tpu as pltpu
from jax.sharding import PartitionSpec as P

NV = 8
SMEM = pl.BlockSpec(memory_space=pltpu.SMEM)
VMEM = pl.BlockSpec(memory_space=pltpu.VMEM)
ANY = pl.BlockSpec(memory_space=pl.ANY)


def pick_t_kernel(home_ref, send_ref, store_ref, out_ref, sem):
    count = out_ref.shape[0]
    per_dev = store_ref.shape[0]

    def start(i, carry):
        row = lax.rem(home_ref[send_ref[i]], per_dev)
        pltpu.make_async_copy(store_ref.at[row], out_ref.at[i], sem).start()
        return carry

    lax.fori_loop(0, count, start, 0, unroll=8)
    pltpu.make_async_copy(out_ref, out_ref, sem).wait()


def pick_t(home, send, store):
    count = send.shape[0]
    _, rows, cols = store.shape
    return pl.pallas_call(
        pick_t_kernel,
        out_shape=jax.ShapeDtypeStruct((count, rows, cols), store.dtype),
        in_specs=[SMEM, SMEM, ANY],
        out_specs=ANY,
        scratch_shapes=[pltpu.SemaphoreType.DMA],
        name="pick_t",
    )(home, send, store)


def form_w_kernel(home_ref, send_ref, ovvo_ref, ovvv_ref, dress_ref, out_ref, formed, sem):
    count = out_ref.shape[0]
    per_dev, rows, cols = formed.shape
    step = 4

    def form(i, carry):
        block = ovvv_ref[pl.ds(i * step, step)].reshape(step * rows, cols)
        dressed = jnp.dot(block, dress_ref[...], preferred_element_type=jnp.float32)
        total = ovvo_ref[pl.ds(i * step, step)].astype(jnp.float32) + dressed.reshape(step, rows, cols)
        formed[pl.ds(i * step, step)] = total.astype(jnp.bfloat16)
        return carry

    lax.fori_loop(0, per_dev // step, form, 0)

    def start(i, carry):
        row = lax.rem(home_ref[send_ref[i]], per_dev)
        pltpu.make_async_copy(formed.at[row], out_ref.at[i], sem).start()
        return carry

    lax.fori_loop(0, count, start, 0, unroll=8)
    pltpu.make_async_copy(out_ref, out_ref, sem).wait()


def form_w(home, send, ovvo, ovvv, dressing):
    count = send.shape[0]
    per_dev, rows, cols = ovvo.shape
    return pl.pallas_call(
        form_w_kernel,
        out_shape=jax.ShapeDtypeStruct((count, rows, cols), jnp.bfloat16),
        in_specs=[SMEM, SMEM, VMEM, VMEM, VMEM],
        out_specs=ANY,
        scratch_shapes=[pltpu.VMEM((per_dev, rows, cols), jnp.bfloat16), pltpu.SemaphoreType.DMA],
        compiler_params=pltpu.CompilerParams(vmem_limit_bytes=32 * 1024 * 1024),
        cost_estimate=pl.CostEstimate(flops=2 * per_dev * rows * cols * cols, bytes_accessed=12 << 20, transcendentals=0),
        name="form_w",
    )(home, send, ovvo, ovvv, dressing)


def products_kernel(task_t_ref, task_w_ref, t_ref, w_ref, out_ref):
    slots, rows, cols = out_ref.shape
    per_slot = task_t_ref.shape[0] // slots
    width = 4

    def slot(s, carry):
        acc = jnp.zeros((rows, cols), jnp.float32)
        for k in range(0, per_slot, width):
            base = s * per_slot + k
            left = jnp.concatenate([t_ref[task_t_ref[base + j]] for j in range(width)], axis=1)
            right = jnp.concatenate([w_ref[task_w_ref[base + j]] for j in range(width)], axis=0)
            acc = acc + jnp.dot(left, right, preferred_element_type=jnp.float32)
        out_ref[s] = acc.astype(out_ref.dtype)
        return carry

    lax.fori_loop(0, slots, slot, 0)


def products(task_t, task_w, t_fetched, w_fetched, slots):
    _, rows, cols = t_fetched.shape
    count = task_t.shape[0]
    return pl.pallas_call(
        products_kernel,
        out_shape=jax.ShapeDtypeStruct((slots, rows, cols), jnp.bfloat16),
        in_specs=[SMEM, SMEM, VMEM, VMEM],
        out_specs=VMEM,
        compiler_params=pltpu.CompilerParams(vmem_limit_bytes=32 * 1024 * 1024),
        cost_estimate=pl.CostEstimate(flops=2 * count * rows * cols * cols, bytes_accessed=7 << 20, transcendentals=0),
        name="products",
    )(task_t, task_w, t_fetched, w_fetched)


def finish_kernel(recv_ref, in_ref, base_ref, right_ref, out_ref, total):
    slots = in_ref.shape[0]
    res_dev = out_ref.shape[0]
    total[...] = jnp.zeros_like(total)

    def add(d, carry):
        row = recv_ref[d]
        total[row] = total[row] + in_ref[d].astype(jnp.float32)
        return carry

    lax.fori_loop(0, slots, add, 0)

    def divide(j, carry):
        denominator = base_ref[j // NV] - right_ref[pl.ds(lax.rem(j, NV), 1), :]
        out_ref[j] = total[j] / denominator
        return carry

    lax.fori_loop(0, res_dev, divide, 0)


def finish(recv, incoming, base, right, res_dev):
    slots, rows, cols = incoming.shape
    return pl.pallas_call(
        finish_kernel,
        out_shape=jax.ShapeDtypeStruct((res_dev, rows, cols), jnp.float32),
        in_specs=[SMEM, VMEM, VMEM, VMEM],
        out_specs=VMEM,
        scratch_shapes=[pltpu.VMEM((res_dev, rows, cols), jnp.float32)],
        compiler_params=pltpu.CompilerParams(vmem_limit_bytes=32 * 1024 * 1024),
        name="finish",
    )(recv, incoming, base, right)


def per_device(
    t2_store,
    ovvo_store,
    ovvv_store,
    dressing,
    t_home,
    t_send,
    w_home,
    w_send,
    task_t,
    task_w,
    recv_rows,
    pair_orbitals,
    eps_occ,
    eps_vir,
):
    tasks_count = lax.axis_size("tasks")
    groups = lax.axis_size("grp")
    tasks_pos = lax.axis_index("tasks")
    group_pos = lax.axis_index("grp")
    tile = t2_store.shape[2]
    slots = task_t.shape[2]
    res_dev = slots // 2

    t_out = pick_t(t_home[0], t_send.reshape(-1), t2_store[0])
    t_in = lax.all_to_all(
        t_out.reshape(tasks_count, -1, tile, tile), "tasks", split_axis=0, concat_axis=0, tiled=True
    ).reshape(-1, tile, tile)
    w_out = form_w(w_home, w_send.reshape(-1), ovvo_store, ovvv_store, dressing)
    w_in = lax.all_to_all(w_out, ("tasks", "grp"), split_axis=0, concat_axis=0, tiled=True)
    partials = products(task_t.reshape(-1), task_w.reshape(-1), t_in, w_in, slots)
    incoming = lax.all_to_all(partials, "tasks", split_axis=0, concat_axis=0, tiled=True)

    per_pair = NV * NV
    group_pairs = tasks_count * res_dev // per_pair
    first = tasks_pos * res_dev
    pair = pair_orbitals[group_pos * group_pairs + first // per_pair]
    occ_sum = eps_occ[pair[0]] + eps_occ[pair[1]]
    vir = eps_vir.reshape(NV, tile)
    left = lax.dynamic_slice_in_dim(vir, first // NV % NV, res_dev // NV, axis=0)
    base = jnp.broadcast_to((occ_sum - left)[:, :, None], (res_dev // NV, tile, tile))
    return finish(recv_rows.reshape(-1), incoming, base, vir, res_dev)[None]


def solution(mesh):
    return jax.shard_map(
        per_device,
        mesh=mesh,
        in_specs=(
            P("grp", "tasks", None, None),
            P(("tasks", "grp"), None, None),
            P(("tasks", "grp"), None, None),
            P(),
            P("grp", None),
            P("grp", "tasks", None, None),
            P(),
            P(("tasks", "grp"), None, None),
            P("grp", "tasks", None, None),
            P("grp", "tasks", None, None),
            P("grp", "tasks", None, None),
            P(),
            P(),
            P(),
        ),
        out_specs=P("grp", "tasks", None, None),
        check_vma=False,
    )
```

```python
import jax
import jax.numpy as jnp
from jax import lax
from jax.experimental import pallas as pl
from jax.experimental.pallas import tpu as pltpu
from jax.sharding import PartitionSpec as P

NV = 8
SMEM = pl.BlockSpec(memory_space=pltpu.SMEM)
VMEM = pl.BlockSpec(memory_space=pltpu.VMEM)
HBM = pl.BlockSpec(memory_space=pltpu.HBM)
CHUNKS = 4
VMEM_BYTES = 48 * 1024 * 1024


def pick_t_kernel(home_ref, send_ref, store_ref, out_ref, stage, sems):
    count = out_ref.shape[0]
    per_dev = store_ref.shape[0]
    cap = send_ref.shape[0]
    chunk = count // CHUNKS
    copies = []
    for c in range(CHUNKS):
        part = pl.ds(c * chunk, chunk)
        for i in range(c * chunk, (c + 1) * chunk):
            stage[i] = store_ref[lax.rem(home_ref[0, send_ref[i % cap, i // cap]], per_dev)]
        copies.append(pltpu.make_async_copy(stage.at[part], out_ref.at[part], sems.at[c]))
        copies[-1].start()
    for copy in copies:
        copy.wait()


def pick_t(home, send, store):
    count = send.shape[0] * send.shape[1]
    _, rows, cols = store.shape
    return pl.pallas_call(
        pick_t_kernel,
        out_shape=jax.ShapeDtypeStruct((count, rows, cols), store.dtype),
        in_specs=[SMEM, SMEM, VMEM],
        out_specs=HBM,
        scratch_shapes=[pltpu.VMEM((count, rows, cols), store.dtype), pltpu.SemaphoreType.DMA((CHUNKS,))],
        compiler_params=pltpu.CompilerParams(vmem_limit_bytes=VMEM_BYTES),
        name="pick_t",
    )(home, send, store)


def form_w_kernel(home_ref, send_ref, ovvo_ref, ovvv_ref, dress_ref, out_ref, formed, stage, sems):
    count = out_ref.shape[0]
    per_dev, rows, cols = formed.shape
    step = 4
    for i in range(0, per_dev, step):
        block = ovvv_ref[i : i + step].reshape(step * rows, cols)
        dressed = jnp.dot(block, dress_ref[...], preferred_element_type=jnp.float32)
        total = ovvo_ref[i : i + step].astype(jnp.float32) + dressed.reshape(step, rows, cols)
        formed[i : i + step] = total.astype(jnp.bfloat16)
    chunk = count // CHUNKS
    copies = []
    for c in range(CHUNKS):

        def pick(i, carry):
            stage[i] = formed[lax.rem(home_ref[send_ref[0, i]], per_dev)]
            return carry

        lax.fori_loop(c * chunk, (c + 1) * chunk, pick, 0, unroll=8)
        part = pl.ds(c * chunk, chunk)
        copies.append(pltpu.make_async_copy(stage.at[part], out_ref.at[part], sems.at[c]))
        copies[-1].start()
    for copy in copies:
        copy.wait()


def form_w(home, send, ovvo, ovvv, dressing):
    count = send.shape[1]
    per_dev, rows, cols = ovvo.shape
    return pl.pallas_call(
        form_w_kernel,
        out_shape=jax.ShapeDtypeStruct((count, rows, cols), jnp.bfloat16),
        in_specs=[SMEM, SMEM, VMEM, VMEM, VMEM],
        out_specs=HBM,
        scratch_shapes=[
            pltpu.VMEM((per_dev, rows, cols), jnp.bfloat16),
            pltpu.VMEM((count, rows, cols), jnp.bfloat16),
            pltpu.SemaphoreType.DMA((CHUNKS,)),
        ],
        compiler_params=pltpu.CompilerParams(vmem_limit_bytes=VMEM_BYTES),
        cost_estimate=pl.CostEstimate(flops=2 * per_dev * rows * cols * cols, bytes_accessed=12 << 20, transcendentals=0),
        name="form_w",
    )(home, send, ovvo, ovvv, dressing)


def products_kernel(task_t_ref, task_w_ref, t_ref, w_ref, out_ref):
    slots, rows, cols = out_ref.shape
    per_slot = task_t_ref.shape[1]
    width, together = 4, 8

    def group(i, carry):
        for u in range(together):
            s = i * together + u
            acc = jnp.zeros((rows, cols), jnp.float32)
            for k in range(0, per_slot, width):
                left = jnp.concatenate([t_ref[task_t_ref[s, k + j]] for j in range(width)], axis=1)
                right = jnp.concatenate([w_ref[task_w_ref[s, k + j]] for j in range(width)], axis=0)
                acc = acc + jnp.dot(left, right, preferred_element_type=jnp.float32)
            out_ref[s] = acc.astype(out_ref.dtype)
        return carry

    lax.fori_loop(0, slots // together, group, 0)


def products(task_t, task_w, t_fetched, w_fetched):
    _, rows, cols = t_fetched.shape
    slots, per_slot = task_t.shape
    return pl.pallas_call(
        products_kernel,
        out_shape=jax.ShapeDtypeStruct((slots, rows, cols), jnp.bfloat16),
        in_specs=[SMEM, SMEM, VMEM, VMEM],
        out_specs=VMEM,
        compiler_params=pltpu.CompilerParams(vmem_limit_bytes=VMEM_BYTES),
        cost_estimate=pl.CostEstimate(flops=2 * slots * per_slot * rows * cols * cols, bytes_accessed=7 << 20, transcendentals=0),
        name="products",
    )(task_t, task_w, t_fetched, w_fetched)


def finish_kernel(recv_ref, in_ref, base_ref, right_ref, out_ref, total):
    slots = in_ref.shape[0]
    res_dev = out_ref.shape[0]
    total[...] = jnp.zeros_like(total)

    def add(d, carry):
        row = recv_ref[0, d]
        total[row] = total[row] + in_ref[d].astype(jnp.float32)
        return carry

    lax.fori_loop(0, slots, add, 0)

    def divide(j, carry):
        denominator = base_ref[j // NV] - right_ref[pl.ds(lax.rem(j, NV), 1), :]
        out_ref[j] = total[j] / denominator
        return carry

    lax.fori_loop(0, res_dev, divide, 0)


def finish(recv, incoming, base, right, res_dev):
    slots, rows, cols = incoming.shape
    return pl.pallas_call(
        finish_kernel,
        out_shape=jax.ShapeDtypeStruct((res_dev, rows, cols), jnp.float32),
        in_specs=[SMEM, VMEM, VMEM, VMEM],
        out_specs=VMEM,
        scratch_shapes=[pltpu.VMEM((res_dev, rows, cols), jnp.float32)],
        compiler_params=pltpu.CompilerParams(vmem_limit_bytes=VMEM_BYTES),
        name="finish",
    )(recv, incoming, base, right)


def per_device(
    t2_store,
    ovvo_store,
    ovvv_store,
    dressing,
    t_home,
    t_send,
    w_home,
    w_send,
    task_t,
    task_w,
    recv_rows,
    pair_orbitals,
    eps_occ,
    eps_vir,
):
    tasks_count = lax.axis_size("tasks")
    groups = lax.axis_size("grp")
    tasks_pos = lax.axis_index("tasks")
    group_pos = lax.axis_index("grp")
    tile = t2_store.shape[2]
    slots = task_t.shape[2]
    res_dev = slots // 2

    t_out = pick_t(t_home, t_send[0, 0].T, t2_store[0])
    t_in = lax.all_to_all(
        t_out.reshape(tasks_count, -1, tile, tile), "tasks", split_axis=0, concat_axis=0, tiled=True
    ).reshape(-1, tile, tile)
    w_out = form_w(w_home, w_send[0].T, ovvo_store, ovvv_store, dressing)
    w_in = lax.all_to_all(w_out, ("tasks", "grp"), split_axis=0, concat_axis=0, tiled=True)
    partials = products(task_t[0, 0], task_w[0, 0], t_in, w_in)
    incoming = lax.all_to_all(partials, "tasks", split_axis=0, concat_axis=0, tiled=True)

    per_pair = NV * NV
    group_pairs = tasks_count * res_dev // per_pair
    first = tasks_pos * res_dev
    pair = pair_orbitals[group_pos * group_pairs + first // per_pair]
    occ_sum = eps_occ[pair[0]] + eps_occ[pair[1]]
    vir = eps_vir.reshape(NV, tile)
    left = lax.dynamic_slice_in_dim(vir, first // NV % NV, res_dev // NV, axis=0)
    base = jnp.broadcast_to((occ_sum - left)[:, :, None], (res_dev // NV, tile, tile))
    return finish(recv_rows[0, 0].T, incoming, base, vir, res_dev)[None]


def solution(mesh):
    return jax.shard_map(
        per_device,
        mesh=mesh,
        in_specs=(
            P("grp", "tasks", None, None),
            P(("tasks", "grp"), None, None),
            P(("tasks", "grp"), None, None),
            P(),
            P("grp", None),
            P("grp", "tasks", None, None),
            P(),
            P(("tasks", "grp"), None, None),
            P("grp", "tasks", None, None),
            P("grp", "tasks", None, None),
            P("grp", "tasks", None, None),
            P(),
            P(),
            P(),
        ),
        out_specs=P("grp", "tasks", None, None),
        check_vma=False,
    )
```

```python
import jax
import jax.numpy as jnp
from jax import lax
from jax.experimental import pallas as pl
from jax.experimental.pallas import tpu as pltpu
from jax.sharding import PartitionSpec as P

NV = 8
SMEM = pl.BlockSpec(memory_space=pltpu.SMEM)
VMEM = pl.BlockSpec(memory_space=pltpu.VMEM)
HBM = pl.BlockSpec(memory_space=pltpu.HBM)
CHUNKS = 4
SIDE = 4
VMEM_BYTES = 16 * 1024 * 1024


def prepare_kernel(t_home_hbm, t_send_hbm, store_hbm, w_home_hbm, w_send_hbm, ovvo_hbm, ovvv_hbm, dress_hbm, *refs):
    t_outs, w_out, scratch = refs[:SIDE], refs[SIDE], refs[SIDE + 1 :]
    t_home, t_send, store, w_home, w_send, ovvo, ovvv, dress, t_stage, formed, w_stage, in_sems, t_sems, w_sems = scratch
    loads = []
    for i, (src, dst) in enumerate(
        (
            (t_home_hbm, t_home),
            (t_send_hbm, t_send),
            (store_hbm, store),
            (ovvv_hbm, ovvv),
            (ovvo_hbm, ovvo),
            (dress_hbm, dress),
            (w_home_hbm, w_home),
            (w_send_hbm, w_send),
        )
    ):
        loads.append(pltpu.make_async_copy(src, dst, in_sems.at[i]))
        loads[-1].start()

    for load in loads[:3]:
        load.wait()
    t_per_dev = store.shape[0]
    cap = t_send.shape[0]
    pos = lax.axis_index("tasks")
    y, x, core = pos // (2 * SIDE), lax.rem(pos // 2, SIDE), lax.rem(pos, 2)
    copies = []
    for first in (1, 2, 3, 0):
        for second in range(SIDE):
            dy = jnp.where(core == 0, first, second)
            dx = jnp.where(core == 0, second, first)
            chip = lax.rem(y + dy, SIDE) * SIDE + lax.rem(x + dx, SIDE)
            for other in range(2):
                there = chip * 2 + (1 - core if other else core)
                for c in range(cap):
                    row = lax.rem(t_home[0, t_send[c, there]], t_per_dev)
                    t_stage[first, (second * 2 + other) * cap + c] = store[row]
        copies.append(pltpu.make_async_copy(t_stage.at[first], t_outs[first], t_sems.at[first]))
        copies[-1].start()

    for load in loads[3:]:
        load.wait()
    w_per_dev, rows, cols = formed.shape
    step = 4
    for i in range(0, w_per_dev, step):
        block = ovvv[i : i + step].reshape(step * rows, cols)
        dressed = jnp.dot(block, dress[...], preferred_element_type=jnp.float32)
        total = ovvo[i : i + step].astype(jnp.float32) + dressed.reshape(step, rows, cols)
        formed[i : i + step] = total.astype(jnp.bfloat16)
    count = w_out.shape[0]
    chunk = count // CHUNKS
    for c in range(CHUNKS):

        def pick(i, carry):
            w_stage[i] = formed[lax.rem(w_home[w_send[0, i]], w_per_dev)]
            return carry

        lax.fori_loop(c * chunk, (c + 1) * chunk, pick, 0, unroll=8)
        part = pl.ds(c * chunk, chunk)
        copies.append(pltpu.make_async_copy(w_stage.at[part], w_out.at[part], w_sems.at[c]))
        copies[-1].start()
    for copy in copies:
        copy.wait()


def prepare(t_home, t_send, store, w_home, w_send, ovvo, ovvv, dressing):
    t_count = t_send.shape[0] * t_send.shape[1]
    w_count = w_send.shape[1]
    w_per_dev, rows, cols = ovvo.shape
    t_part = jax.ShapeDtypeStruct((t_count // SIDE, rows, cols), store.dtype)
    w_all = jax.ShapeDtypeStruct((w_count, rows, cols), jnp.bfloat16)
    return pl.pallas_call(
        prepare_kernel,
        out_shape=[t_part] * SIDE + [w_all],
        in_specs=[HBM] * 8,
        out_specs=[HBM] * (SIDE + 1),
        scratch_shapes=[
            pltpu.SMEM(t_home.shape, t_home.dtype),
            pltpu.SMEM(t_send.shape, t_send.dtype),
            pltpu.VMEM(store.shape, store.dtype),
            pltpu.SMEM(w_home.shape, w_home.dtype),
            pltpu.SMEM(w_send.shape, w_send.dtype),
            pltpu.VMEM(ovvo.shape, ovvo.dtype),
            pltpu.VMEM(ovvv.shape, ovvv.dtype),
            pltpu.VMEM(dressing.shape, dressing.dtype),
            pltpu.VMEM((SIDE,) + t_part.shape, store.dtype),
            pltpu.VMEM((w_per_dev, rows, cols), jnp.bfloat16),
            pltpu.VMEM(w_all.shape, jnp.bfloat16),
            pltpu.SemaphoreType.DMA((8,)),
            pltpu.SemaphoreType.DMA((SIDE,)),
            pltpu.SemaphoreType.DMA((CHUNKS,)),
        ],
        compiler_params=pltpu.CompilerParams(vmem_limit_bytes=62 * 1024 * 1024),
        name="prepare",
    )(t_home, t_send, store, w_home, w_send, ovvo, ovvv, dressing)


def regroup_kernel(*refs):
    ins, outs, sems = refs[:SIDE], refs[SIDE:-1], refs[-1]
    cap = ins[0].shape[0] // (2 * SIDE)
    copies = []
    for second in (2, 1, 3, 0):
        for which in (1, 0):
            for first in range(SIDE):
                src = ins[first].at[pl.ds((second * 2 + which) * cap, cap)]
                out, base = (outs[-1], (1 - which) * SIDE * cap) if second == 2 else (outs[PLACE[which, second]], 0)
                dst = out.at[pl.ds(base + first * cap, cap)]
                copies.append(pltpu.make_async_copy(src, dst, sems.at[which, second, first]))
                copies[-1].start()
    for copy in copies:
        copy.wait()


PLACE = {(0, 0): 0, (0, 1): 1, (0, 3): 2, (1, 0): 3, (1, 1): 4, (1, 3): 5}


def regroup(parts):
    count, rows, cols = parts[0].shape
    part = jax.ShapeDtypeStruct((count // 2, rows, cols), parts[0].dtype)
    return pl.pallas_call(
        regroup_kernel,
        out_shape=[part] * 6 + [jax.ShapeDtypeStruct(parts[0].shape, parts[0].dtype)],
        in_specs=[VMEM] * SIDE,
        out_specs=[HBM] * 7,
        scratch_shapes=[pltpu.SemaphoreType.DMA((2, SIDE, SIDE))],
        compiler_params=pltpu.CompilerParams(vmem_limit_bytes=VMEM_BYTES),
        cost_estimate=pl.CostEstimate(flops=10**11, bytes_accessed=4 << 20, transcendentals=0),
        name="regroup",
    )(*parts)


def shift(k, first_axis):
    pairs = []
    for y in range(SIDE):
        for x in range(SIDE):
            for core in range(2):
                ty, tx = ((y + k) % SIDE, x) if core == first_axis else (y, (x + k) % SIDE)
                pairs.append(((y * SIDE + x) * 2 + core, (ty * SIDE + tx) * 2 + core))
    return pairs


def move(part, k, first_axis):
    return lax.ppermute(part, "tasks", shift(k, first_axis))


def swap_cores(part):
    return lax.ppermute(part, "tasks", [(i, i ^ 1) for i in range(2 * SIDE * SIDE)])


def fetch_t(parts, w_fetched):
    parts = [parts[0]] + [move(parts[k], k, 0) for k in range(1, SIDE)]
    same0, same1, same3, other0, other1, other3, both2 = regroup(parts)
    other0, other1, other3 = swap_cores(other0), swap_cores(other1), swap_cores(other3)
    same1, same3, other0, other1, other3, both2 = lax.optimization_barrier(
        (same1, same3, other0, other1, other3, both2)
    )
    both2 = move(both2, 2, 1)
    same1, other1 = move(same1, 1, 1), move(other1, 1, 0)
    same3, other3 = move(same3, 3, 1), move(other3, 3, 0)
    swapped = both2[: both2.shape[0] // 2]
    w_fetched, swapped = lax.optimization_barrier((w_fetched, swapped))
    other2 = swap_cores(swapped)
    return (same0, same1, both2, same3, other0, other1, other2, other3), w_fetched


def slot_places(task_t, pos, cap):
    y, x, core = pos // (2 * SIDE), pos // 2 % SIDE, pos % 2
    owner = task_t // cap
    dy = (y - owner // (2 * SIDE)) % SIDE
    dx = (x - owner // 2 % SIDE) % SIDE
    first = jnp.where(owner % 2 == 0, dy, dx)
    second = jnp.where(owner % 2 == 0, dx, dy)
    group = jnp.where(owner % 2 == core, second, second + SIDE)
    return (group * SIDE + first) * cap + task_t % cap


def products_kernel(task_ref, w_ref, *refs):
    parts, (out_ref, t_ref, sems) = refs[: 2 * SIDE], refs[2 * SIDE :]
    copies = []
    count = parts[0].shape[0]
    for i, part in enumerate(parts):
        part = part.at[pl.ds(part.shape[0] - count, count)]
        copies.append(pltpu.make_async_copy(part, t_ref.at[pl.ds(i * count, count)], sems.at[i]))
    for copy in copies:
        copy.start()
    for copy in copies:
        copy.wait()
    slots, rows, cols = out_ref.shape
    per_slot = task_ref.shape[2]
    width, together = 4, 8

    def group(i, carry):
        for u in range(together):
            s = i * together + u
            acc = jnp.zeros((rows, cols), jnp.float32)
            for k in range(0, per_slot, width):
                left = jnp.concatenate([t_ref[task_ref[0, s, k + j]] for j in range(width)], axis=1)
                right = jnp.concatenate([w_ref[task_ref[1, s, k + j]] for j in range(width)], axis=0)
                acc = acc + jnp.dot(left, right, preferred_element_type=jnp.float32)
            out_ref[s] = acc.astype(out_ref.dtype)
        return carry

    lax.fori_loop(0, slots // together, group, 0)


def products(tasks, t_parts, w_fetched):
    count, rows, cols = t_parts[0].shape
    _, slots, per_slot = tasks.shape
    return pl.pallas_call(
        products_kernel,
        out_shape=jax.ShapeDtypeStruct((slots, rows, cols), jnp.bfloat16),
        in_specs=[SMEM, VMEM] + [HBM] * (2 * SIDE),
        out_specs=VMEM,
        scratch_shapes=[
            pltpu.VMEM((2 * SIDE * count, rows, cols), jnp.bfloat16),
            pltpu.SemaphoreType.DMA((2 * SIDE,)),
        ],
        compiler_params=pltpu.CompilerParams(vmem_limit_bytes=VMEM_BYTES),
        cost_estimate=pl.CostEstimate(flops=2 * slots * per_slot * rows * cols * cols, bytes_accessed=7 << 20, transcendentals=0),
        name="products",
    )(tasks, w_fetched, *t_parts)


def finish_kernel(slot_ref, in_ref, inverse_ref, out_hbm, out_ref, sems):
    res_dev = out_ref.shape[0]
    chunk = res_dev // CHUNKS
    copies = []
    for c in range(CHUNKS):
        for j in range(c * chunk, (c + 1) * chunk):
            total = in_ref[slot_ref[0, j]].astype(jnp.float32) + in_ref[slot_ref[1, j]].astype(jnp.float32)
            out_ref[j] = total * inverse_ref[j]
        part = pl.ds(c * chunk, chunk)
        copies.append(pltpu.make_async_copy(out_ref.at[part], out_hbm.at[part], sems.at[c]))
        copies[-1].start()
    for copy in copies:
        copy.wait()


def finish(pair_slots, incoming, inverse):
    return pl.pallas_call(
        finish_kernel,
        out_shape=jax.ShapeDtypeStruct(inverse.shape, jnp.float32),
        in_specs=[SMEM, VMEM, VMEM],
        out_specs=HBM,
        scratch_shapes=[pltpu.VMEM(inverse.shape, jnp.float32), pltpu.SemaphoreType.DMA((CHUNKS,))],
        compiler_params=pltpu.CompilerParams(vmem_limit_bytes=VMEM_BYTES),
        name="finish",
    )(pair_slots, incoming, inverse)


def per_device(
    t2_store,
    ovvo_store,
    ovvv_store,
    dressing,
    t_home,
    t_send,
    w_home,
    w_send,
    task_t,
    task_w,
    recv_rows,
    pair_orbitals,
    eps_occ,
    eps_vir,
):
    tasks_count = lax.axis_size("tasks")
    groups = lax.axis_size("grp")
    tasks_pos = lax.axis_index("tasks")
    group_pos = lax.axis_index("grp")
    tile = t2_store.shape[2]
    slots = task_t.shape[2]
    res_dev = slots // 2

    *t_out, w_out = prepare(
        t_home, t_send[0, 0].T, t2_store[0], w_home, w_send[0].T, ovvo_store, ovvv_store, dressing
    )
    w_in = lax.all_to_all(w_out, ("tasks", "grp"), split_axis=0, concat_axis=0, tiled=True)
    t_parts, w_in = fetch_t(t_out, w_in)
    tasks = jnp.stack([slot_places(task_t[0, 0], tasks_pos, t_send.shape[3]), task_w[0, 0]])
    partials = products(tasks, t_parts, w_in)
    incoming = lax.all_to_all(partials, "tasks", split_axis=0, concat_axis=0, tiled=True)

    per_pair = NV * NV
    group_pairs = tasks_count * res_dev // per_pair
    first = tasks_pos * res_dev
    pair = pair_orbitals[group_pos * group_pairs + first // per_pair]
    occ_sum = eps_occ[pair[0]] + eps_occ[pair[1]]
    vir = eps_vir.reshape(NV, tile)
    left = lax.dynamic_slice_in_dim(vir, first // NV % NV, res_dev // NV, axis=0)
    base = occ_sum - left[:, None, :, None]
    inverse = (1.0 / (base - vir[None, :, None, :])).reshape(res_dev, tile, tile)
    named = recv_rows[0, 0].T == jnp.arange(res_dev, dtype=jnp.int32)[:, None]
    slot = jnp.arange(slots, dtype=jnp.int32)[None, :]
    low = jnp.min(jnp.where(named, slot, slots - 1), axis=1)
    high = jnp.max(jnp.where(named, slot, 0), axis=1)
    return finish(jnp.stack([low, high]), incoming, inverse)[None]


def solution(mesh):
    return jax.shard_map(
        per_device,
        mesh=mesh,
        in_specs=(
            P("grp", "tasks", None, None),
            P(("tasks", "grp"), None, None),
            P(("tasks", "grp"), None, None),
            P(),
            P("grp", None),
            P("grp", "tasks", None, None),
            P(),
            P(("tasks", "grp"), None, None),
            P("grp", "tasks", None, None),
            P("grp", "tasks", None, None),
            P("grp", "tasks", None, None),
            P(),
            P(),
            P(),
        ),
        out_specs=P("grp", "tasks", None, None),
        check_vma=False,
    )
```

```python
import jax
import jax.numpy as jnp
from jax import lax
from jax.experimental import pallas as pl
from jax.experimental.pallas import tpu as pltpu
from jax.sharding import PartitionSpec as P

NV = 8
SMEM = pl.BlockSpec(memory_space=pltpu.SMEM)
VMEM = pl.BlockSpec(memory_space=pltpu.VMEM)
HBM = pl.BlockSpec(memory_space=pltpu.HBM)
CHUNKS = 4
SIDE = 4
VMEM_MOST = 62 * 1024 * 1024
VMEM_BYTES = 16 * 1024 * 1024


def prepare_kernel(t_home_hbm, t_send_hbm, store_hbm, w_home_hbm, w_send_hbm, ovvo_hbm, ovvv_hbm, dress_hbm, *refs):
    t_outs, w_out, scratch = refs[:SIDE], refs[SIDE], refs[SIDE + 1 :]
    t_home, t_send, store, w_home, w_send, ovvo, ovvv, dress, t_stage, formed, w_stage, in_sems, t_sems, w_sems = scratch
    loads = []
    for i, (src, dst) in enumerate(
        (
            (t_home_hbm, t_home),
            (t_send_hbm, t_send),
            (store_hbm, store),
            (ovvv_hbm, ovvv),
            (ovvo_hbm, ovvo),
            (dress_hbm, dress),
            (w_home_hbm, w_home),
            (w_send_hbm, w_send),
        )
    ):
        loads.append(pltpu.make_async_copy(src, dst, in_sems.at[i]))
        loads[-1].start()

    for load in loads[:3]:
        load.wait()
    t_per_dev = store.shape[0]
    cap = t_send.shape[0]
    pos = lax.axis_index("tasks")
    y, x, core = pos // (2 * SIDE), lax.rem(pos // 2, SIDE), lax.rem(pos, 2)
    copies = []
    for first in (1, 2, 3, 0):
        for second in range(SIDE):
            dy = jnp.where(core == 0, first, second)
            dx = jnp.where(core == 0, second, first)
            chip = lax.rem(y + dy, SIDE) * SIDE + lax.rem(x + dx, SIDE)
            for other in range(2):
                there = chip * 2 + (1 - core if other else core)
                for c in range(cap):
                    row = lax.rem(t_home[0, t_send[c, there]], t_per_dev)
                    t_stage[first, (second * 2 + other) * cap + c] = store[row]
        copies.append(pltpu.make_async_copy(t_stage.at[first], t_outs[first], t_sems.at[first]))
        copies[-1].start()

    for load in loads[3:]:
        load.wait()
    w_per_dev, rows, cols = formed.shape
    step = 4
    for i in range(0, w_per_dev, step):
        block = ovvv[i : i + step].reshape(step * rows, cols)
        dressed = jnp.dot(block, dress[...], preferred_element_type=jnp.float32)
        total = ovvo[i : i + step].astype(jnp.float32) + dressed.reshape(step, rows, cols)
        formed[i : i + step] = total.astype(jnp.bfloat16)
    count = w_out.shape[0]
    chunk = count // CHUNKS
    for c in range(CHUNKS):

        def pick(i, carry):
            w_stage[i] = formed[lax.rem(w_home[w_send[0, i]], w_per_dev)]
            return carry

        lax.fori_loop(c * chunk, (c + 1) * chunk, pick, 0, unroll=8)
        part = pl.ds(c * chunk, chunk)
        copies.append(pltpu.make_async_copy(w_stage.at[part], w_out.at[part], w_sems.at[c]))
        copies[-1].start()
    for copy in copies:
        copy.wait()


def prepare(t_home, t_send, store, w_home, w_send, ovvo, ovvv, dressing):
    t_count = t_send.shape[0] * t_send.shape[1]
    w_count = w_send.shape[1]
    w_per_dev, rows, cols = ovvo.shape
    t_part = jax.ShapeDtypeStruct((t_count // SIDE, rows, cols), store.dtype)
    w_all = jax.ShapeDtypeStruct((w_count, rows, cols), jnp.bfloat16)
    return pl.pallas_call(
        prepare_kernel,
        out_shape=[t_part] * SIDE + [w_all],
        in_specs=[HBM] * 8,
        out_specs=[HBM] * (SIDE + 1),
        scratch_shapes=[
            pltpu.SMEM(t_home.shape, t_home.dtype),
            pltpu.SMEM(t_send.shape, t_send.dtype),
            pltpu.VMEM(store.shape, store.dtype),
            pltpu.SMEM(w_home.shape, w_home.dtype),
            pltpu.SMEM(w_send.shape, w_send.dtype),
            pltpu.VMEM(ovvo.shape, ovvo.dtype),
            pltpu.VMEM(ovvv.shape, ovvv.dtype),
            pltpu.VMEM(dressing.shape, dressing.dtype),
            pltpu.VMEM((SIDE,) + t_part.shape, store.dtype),
            pltpu.VMEM((w_per_dev, rows, cols), jnp.bfloat16),
            pltpu.VMEM(w_all.shape, jnp.bfloat16),
            pltpu.SemaphoreType.DMA((8,)),
            pltpu.SemaphoreType.DMA((SIDE,)),
            pltpu.SemaphoreType.DMA((CHUNKS,)),
        ],
        compiler_params=pltpu.CompilerParams(vmem_limit_bytes=VMEM_MOST),
        name="prepare",
    )(t_home, t_send, store, w_home, w_send, ovvo, ovvv, dressing)


def regroup_kernel(*refs):
    ins, outs, sems = refs[:SIDE], refs[SIDE:-1], refs[-1]
    cap = ins[0].shape[0] // (2 * SIDE)
    copies = []
    for second in (2, 1, 3, 0):
        for which in (1, 0):
            for first in range(SIDE):
                src = ins[first].at[pl.ds((second * 2 + which) * cap, cap)]
                out, base = (outs[-1], (1 - which) * SIDE * cap) if second == 2 else (outs[PLACE[which, second]], 0)
                dst = out.at[pl.ds(base + first * cap, cap)]
                copies.append(pltpu.make_async_copy(src, dst, sems.at[which, second, first]))
                copies[-1].start()
    for copy in copies:
        copy.wait()


PLACE = {(0, 0): 0, (0, 1): 1, (0, 3): 2, (1, 0): 3, (1, 1): 4, (1, 3): 5}


def regroup(parts):
    count, rows, cols = parts[0].shape
    part = jax.ShapeDtypeStruct((count // 2, rows, cols), parts[0].dtype)
    return pl.pallas_call(
        regroup_kernel,
        out_shape=[part] * 6 + [jax.ShapeDtypeStruct(parts[0].shape, parts[0].dtype)],
        in_specs=[VMEM] * SIDE,
        out_specs=[HBM] * 7,
        scratch_shapes=[pltpu.SemaphoreType.DMA((2, SIDE, SIDE))],
        compiler_params=pltpu.CompilerParams(vmem_limit_bytes=VMEM_MOST),
        cost_estimate=pl.CostEstimate(flops=10**11, bytes_accessed=4 << 20, transcendentals=0),
        name="regroup",
    )(*parts)


def shift(k, first_axis):
    pairs = []
    for y in range(SIDE):
        for x in range(SIDE):
            for core in range(2):
                ty, tx = ((y + k) % SIDE, x) if core == first_axis else (y, (x + k) % SIDE)
                pairs.append(((y * SIDE + x) * 2 + core, (ty * SIDE + tx) * 2 + core))
    return pairs


def move(part, k, first_axis):
    return lax.ppermute(part, "tasks", shift(k, first_axis))


def swap_cores(part):
    return lax.ppermute(part, "tasks", [(i, i ^ 1) for i in range(2 * SIDE * SIDE)])


def fetch_t(parts, w_fetched):
    parts = [parts[0]] + [move(parts[k], k, 0) for k in range(1, SIDE)]
    same0, same1, same3, other0, other1, other3, both2 = regroup(parts)
    other0, other1, other3 = swap_cores(other0), swap_cores(other1), swap_cores(other3)
    same1, same3, other0, other1, other3, both2 = lax.optimization_barrier(
        (same1, same3, other0, other1, other3, both2)
    )
    both2 = move(both2, 2, 1)
    same1, other1 = move(same1, 1, 1), move(other1, 1, 0)
    same3, other3 = move(same3, 3, 1), move(other3, 3, 0)
    w_fetched, both2 = lax.optimization_barrier((stage(w_fetched), both2))
    other2 = swap_cores(both2[: both2.shape[0] // 2])
    return (same0, same1, both2, same3, other0, other1, other2, other3), w_fetched


def stage_kernel(hbm, out_ref, sems):
    chunk = hbm.shape[0] // CHUNKS
    copies = []
    for c in range(CHUNKS):
        part = pl.ds(c * chunk, chunk)
        copies.append(pltpu.make_async_copy(hbm.at[part], out_ref.at[part], sems.at[c]))
        copies[-1].start()
    for copy in copies:
        copy.wait()


def stage(value):
    return pl.pallas_call(
        stage_kernel,
        out_shape=jax.ShapeDtypeStruct(value.shape, value.dtype),
        in_specs=[HBM],
        out_specs=VMEM,
        scratch_shapes=[pltpu.SemaphoreType.DMA((CHUNKS,))],
        compiler_params=pltpu.CompilerParams(vmem_limit_bytes=VMEM_BYTES),
        cost_estimate=pl.CostEstimate(flops=5*10**9, bytes_accessed=8 << 20, transcendentals=0),
        name="stage",
    )(value)


def slot_places(task_t, pos, cap):
    y, x, core = pos // (2 * SIDE), pos // 2 % SIDE, pos % 2
    owner = task_t // cap
    dy = (y - owner // (2 * SIDE)) % SIDE
    dx = (x - owner // 2 % SIDE) % SIDE
    first = jnp.where(owner % 2 == 0, dy, dx)
    second = jnp.where(owner % 2 == 0, dx, dy)
    group = jnp.where(owner % 2 == core, second, second + SIDE)
    return (group * SIDE + first) * cap + task_t % cap


def products_kernel(task_ref, w_ref, *refs):
    parts, (out_ref, t_ref, sems) = refs[: 2 * SIDE], refs[2 * SIDE :]
    copies = []
    count = parts[0].shape[0]
    for i, part in enumerate(parts):
        part = part.at[pl.ds(part.shape[0] - count, count)]
        copies.append(pltpu.make_async_copy(part, t_ref.at[pl.ds(i * count, count)], sems.at[i]))
    for copy in copies:
        copy.start()
    for copy in copies:
        copy.wait()
    slots, rows, cols = out_ref.shape
    per_slot = task_ref.shape[2]
    width, together = 4, 8

    def group(i, carry):
        for u in range(together):
            s = i * together + u
            acc = jnp.zeros((rows, cols), jnp.float32)
            for k in range(0, per_slot, width):
                left = jnp.concatenate([t_ref[task_ref[0, s, k + j]] for j in range(width)], axis=1)
                right = jnp.concatenate([w_ref[task_ref[1, s, k + j]] for j in range(width)], axis=0)
                acc = acc + jnp.dot(left, right, preferred_element_type=jnp.float32)
            out_ref[s] = acc.astype(out_ref.dtype)
        return carry

    lax.fori_loop(0, slots // together, group, 0)


def products(tasks, t_parts, w_fetched):
    count, rows, cols = t_parts[0].shape
    _, slots, per_slot = tasks.shape
    return pl.pallas_call(
        products_kernel,
        out_shape=jax.ShapeDtypeStruct((slots, rows, cols), jnp.bfloat16),
        in_specs=[SMEM, VMEM] + [HBM] * (2 * SIDE),
        out_specs=VMEM,
        scratch_shapes=[
            pltpu.VMEM((2 * SIDE * count, rows, cols), jnp.bfloat16),
            pltpu.SemaphoreType.DMA((2 * SIDE,)),
        ],
        compiler_params=pltpu.CompilerParams(vmem_limit_bytes=VMEM_BYTES),
        cost_estimate=pl.CostEstimate(flops=2 * slots * per_slot * rows * cols * cols, bytes_accessed=7 << 20, transcendentals=0),
        name="products",
    )(tasks, w_fetched, *t_parts)


def finish_kernel(slot_ref, in_ref, inverse_ref, out_hbm, out_ref, sems):
    res_dev = out_ref.shape[0]
    chunk = res_dev // CHUNKS
    copies = []
    for c in range(CHUNKS):
        for j in range(c * chunk, (c + 1) * chunk):
            total = in_ref[slot_ref[0, j]].astype(jnp.float32) + in_ref[slot_ref[1, j]].astype(jnp.float32)
            out_ref[j] = total * inverse_ref[j]
        part = pl.ds(c * chunk, chunk)
        copies.append(pltpu.make_async_copy(out_ref.at[part], out_hbm.at[part], sems.at[c]))
        copies[-1].start()
    for copy in copies:
        copy.wait()


def finish(pair_slots, incoming, inverse):
    return pl.pallas_call(
        finish_kernel,
        out_shape=jax.ShapeDtypeStruct(inverse.shape, jnp.float32),
        in_specs=[SMEM, VMEM, VMEM],
        out_specs=HBM,
        scratch_shapes=[pltpu.VMEM(inverse.shape, jnp.float32), pltpu.SemaphoreType.DMA((CHUNKS,))],
        compiler_params=pltpu.CompilerParams(vmem_limit_bytes=VMEM_BYTES),
        name="finish",
    )(pair_slots, incoming, inverse)


def per_device(
    t2_store,
    ovvo_store,
    ovvv_store,
    dressing,
    t_home,
    t_send,
    w_home,
    w_send,
    task_t,
    task_w,
    recv_rows,
    pair_orbitals,
    eps_occ,
    eps_vir,
):
    tasks_count = lax.axis_size("tasks")
    groups = lax.axis_size("grp")
    tasks_pos = lax.axis_index("tasks")
    group_pos = lax.axis_index("grp")
    tile = t2_store.shape[2]
    slots = task_t.shape[2]
    res_dev = slots // 2

    *t_out, w_out = prepare(
        t_home, t_send[0, 0].T, t2_store[0], w_home, w_send[0].T, ovvo_store, ovvv_store, dressing
    )
    w_in = lax.all_to_all(w_out, ("tasks", "grp"), split_axis=0, concat_axis=0, tiled=True)
    t_parts, w_in = fetch_t(t_out, w_in)
    tasks = jnp.stack([slot_places(task_t[0, 0], tasks_pos, t_send.shape[3]), task_w[0, 0]])
    partials = products(tasks, t_parts, w_in)
    incoming = lax.all_to_all(partials, "tasks", split_axis=0, concat_axis=0, tiled=True)

    per_pair = NV * NV
    group_pairs = tasks_count * res_dev // per_pair
    first = tasks_pos * res_dev
    pair = pair_orbitals[group_pos * group_pairs + first // per_pair]
    occ_sum = eps_occ[pair[0]] + eps_occ[pair[1]]
    vir = eps_vir.reshape(NV, tile)
    left = lax.dynamic_slice_in_dim(vir, first // NV % NV, res_dev // NV, axis=0)
    base = occ_sum - left[:, None, :, None]
    inverse = (1.0 / (base - vir[None, :, None, :])).reshape(res_dev, tile, tile)
    named = recv_rows[0, 0].T == jnp.arange(res_dev, dtype=jnp.int32)[:, None]
    slot = jnp.arange(slots, dtype=jnp.int32)[None, :]
    low = jnp.min(jnp.where(named, slot, slots - 1), axis=1)
    high = jnp.max(jnp.where(named, slot, 0), axis=1)
    return finish(jnp.stack([low, high]), incoming, inverse)[None]


def solution(mesh):
    return jax.shard_map(
        per_device,
        mesh=mesh,
        in_specs=(
            P("grp", "tasks", None, None),
            P(("tasks", "grp"), None, None),
            P(("tasks", "grp"), None, None),
            P(),
            P("grp", None),
            P("grp", "tasks", None, None),
            P(),
            P(("tasks", "grp"), None, None),
            P("grp", "tasks", None, None),
            P("grp", "tasks", None, None),
            P("grp", "tasks", None, None),
            P(),
            P(),
            P(),
        ),
        out_specs=P("grp", "tasks", None, None),
        check_vma=False,
    )
```

```python
import jax
import jax.numpy as jnp
from jax import lax
from jax.experimental import pallas as pl
from jax.experimental.pallas import tpu as pltpu
from jax.sharding import PartitionSpec as P

NV = 8
SMEM = pl.BlockSpec(memory_space=pltpu.SMEM)
VMEM = pl.BlockSpec(memory_space=pltpu.VMEM)
HBM = pl.BlockSpec(memory_space=pltpu.HBM)
CHUNKS = 4
SIDE = 4
VMEM_MOST = 62 * 1024 * 1024
VMEM_BYTES = 16 * 1024 * 1024


def prepare_kernel(t_home_hbm, t_send_hbm, store_hbm, w_home_hbm, w_send_hbm, ovvo_hbm, ovvv_hbm, dress_hbm, *refs):
    t_outs, w_out, scratch = refs[:SIDE], refs[SIDE], refs[SIDE + 1 :]
    t_home, t_send, store, w_home, w_send, ovvo, ovvv, dress, t_stage, formed, w_stage, in_sems, t_sems, w_sems = scratch
    w_per_dev, rows, cols = formed.shape
    half = w_per_dev // 2
    pairs = [(dress_hbm, dress)]
    for c in range(2):
        part = pl.ds(c * half, half)
        pairs += [(ovvv_hbm.at[part], ovvv.at[part]), (ovvo_hbm.at[part], ovvo.at[part])]
    pairs += [(w_home_hbm, w_home), (w_send_hbm, w_send), (t_home_hbm, t_home), (t_send_hbm, t_send)]
    pairs += [(store_hbm, store)]
    loads = []
    for i, (src, dst) in enumerate(pairs):
        loads.append(pltpu.make_async_copy(src, dst, in_sems.at[i]))
        loads[-1].start()

    step = 4
    loads[0].wait()
    for c in range(2):
        loads[1 + 2 * c].wait()
        loads[2 + 2 * c].wait()
        for i in range(c * half, (c + 1) * half, step):
            block = ovvv[i : i + step].reshape(step * rows, cols)
            dressed = jnp.dot(block, dress[...], preferred_element_type=jnp.float32)
            total = ovvo[i : i + step].astype(jnp.float32) + dressed.reshape(step, rows, cols)
            formed[i : i + step] = total.astype(jnp.bfloat16)
    for load in loads[5:7]:
        load.wait()
    copies = []
    count = w_out.shape[0]
    chunk = count // CHUNKS
    for c in range(CHUNKS):

        def pick(i, carry):
            w_stage[i] = formed[lax.rem(w_home[w_send[0, i]], w_per_dev)]
            return carry

        lax.fori_loop(c * chunk, (c + 1) * chunk, pick, 0, unroll=8)
        part = pl.ds(c * chunk, chunk)
        copies.append(pltpu.make_async_copy(w_stage.at[part], w_out.at[part], w_sems.at[c]))
        copies[-1].start()

    for load in loads[7:]:
        load.wait()
    t_per_dev = store.shape[0]
    cap = t_send.shape[0]
    pos = lax.axis_index("tasks")
    y, x, core = pos // (2 * SIDE), lax.rem(pos // 2, SIDE), lax.rem(pos, 2)
    for first in (1, 2, 3, 0):
        for second in range(SIDE):
            dy = jnp.where(core == 0, first, second)
            dx = jnp.where(core == 0, second, first)
            chip = lax.rem(y + dy, SIDE) * SIDE + lax.rem(x + dx, SIDE)
            for other in range(2):
                there = chip * 2 + (1 - core if other else core)
                for c in range(cap):
                    row = lax.rem(t_home[0, t_send[c, there]], t_per_dev)
                    t_stage[first, (second * 2 + other) * cap + c] = store[row]
        copies.append(pltpu.make_async_copy(t_stage.at[first], t_outs[first], t_sems.at[first]))
        copies[-1].start()
    for copy in copies:
        copy.wait()


def prepare(t_home, t_send, store, w_home, w_send, ovvo, ovvv, dressing):
    t_count = t_send.shape[0] * t_send.shape[1]
    w_count = w_send.shape[1]
    w_per_dev, rows, cols = ovvo.shape
    t_part = jax.ShapeDtypeStruct((t_count // SIDE, rows, cols), store.dtype)
    w_all = jax.ShapeDtypeStruct((w_count, rows, cols), jnp.bfloat16)
    return pl.pallas_call(
        prepare_kernel,
        out_shape=[t_part] * SIDE + [w_all],
        in_specs=[HBM] * 8,
        out_specs=[HBM] * (SIDE + 1),
        scratch_shapes=[
            pltpu.SMEM(t_home.shape, t_home.dtype),
            pltpu.SMEM(t_send.shape, t_send.dtype),
            pltpu.VMEM(store.shape, store.dtype),
            pltpu.SMEM(w_home.shape, w_home.dtype),
            pltpu.SMEM(w_send.shape, w_send.dtype),
            pltpu.VMEM(ovvo.shape, ovvo.dtype),
            pltpu.VMEM(ovvv.shape, ovvv.dtype),
            pltpu.VMEM(dressing.shape, dressing.dtype),
            pltpu.VMEM((SIDE,) + t_part.shape, store.dtype),
            pltpu.VMEM((w_per_dev, rows, cols), jnp.bfloat16),
            pltpu.VMEM(w_all.shape, jnp.bfloat16),
            pltpu.SemaphoreType.DMA((10,)),
            pltpu.SemaphoreType.DMA((SIDE,)),
            pltpu.SemaphoreType.DMA((CHUNKS,)),
        ],
        compiler_params=pltpu.CompilerParams(vmem_limit_bytes=VMEM_MOST),
        name="prepare",
    )(t_home, t_send, store, w_home, w_send, ovvo, ovvv, dressing)


def regroup_kernel(*refs):
    ins, outs, sems = refs[:SIDE], refs[SIDE:-1], refs[-1]
    cap = ins[0].shape[0] // (2 * SIDE)
    copies = []
    for second in (2, 1, 3, 0):
        for which in (1, 0):
            for first in range(SIDE):
                src = ins[first].at[pl.ds((second * 2 + which) * cap, cap)]
                out, base = (outs[-1], (1 - which) * SIDE * cap) if second == 2 else (outs[PLACE[which, second]], 0)
                dst = out.at[pl.ds(base + first * cap, cap)]
                copies.append(pltpu.make_async_copy(src, dst, sems.at[which, second, first]))
                copies[-1].start()
    for copy in copies:
        copy.wait()


PLACE = {(0, 0): 0, (0, 1): 1, (0, 3): 2, (1, 0): 3, (1, 1): 4, (1, 3): 5}


def regroup(parts):
    count, rows, cols = parts[0].shape
    part = jax.ShapeDtypeStruct((count // 2, rows, cols), parts[0].dtype)
    return pl.pallas_call(
        regroup_kernel,
        out_shape=[part] * 6 + [jax.ShapeDtypeStruct(parts[0].shape, parts[0].dtype)],
        in_specs=[VMEM] * SIDE,
        out_specs=[HBM] * 7,
        scratch_shapes=[pltpu.SemaphoreType.DMA((2, SIDE, SIDE))],
        compiler_params=pltpu.CompilerParams(vmem_limit_bytes=VMEM_MOST),
        cost_estimate=pl.CostEstimate(flops=10**11, bytes_accessed=4 << 20, transcendentals=0),
        name="regroup",
    )(*parts)


def shift(k, first_axis):
    pairs = []
    for y in range(SIDE):
        for x in range(SIDE):
            for core in range(2):
                ty, tx = ((y + k) % SIDE, x) if core == first_axis else (y, (x + k) % SIDE)
                pairs.append(((y * SIDE + x) * 2 + core, (ty * SIDE + tx) * 2 + core))
    return pairs


def move(part, k, first_axis):
    return lax.ppermute(part, "tasks", shift(k, first_axis))


def swap_cores(part):
    return lax.ppermute(part, "tasks", [(i, i ^ 1) for i in range(2 * SIDE * SIDE)])


def fetch_t(parts, w_fetched):
    parts = [parts[0]] + [move(parts[k], k, 0) for k in range(1, SIDE)]
    same0, same1, same3, other0, other1, other3, both2 = regroup(parts)
    other0, other1, other3 = swap_cores(other0), swap_cores(other1), swap_cores(other3)
    same1, same3, other0, other1, other3, both2 = lax.optimization_barrier(
        (same1, same3, other0, other1, other3, both2)
    )
    both2 = move(both2, 2, 1)
    same1, other1 = move(same1, 1, 1), move(other1, 1, 0)
    same3, other3 = move(same3, 3, 1), move(other3, 3, 0)
    w_fetched, both2 = lax.optimization_barrier((stage(w_fetched), both2))
    other2 = swap_cores(both2[: both2.shape[0] // 2])
    return (same0, same1, both2, same3, other0, other1, other2, other3), w_fetched


def stage_kernel(hbm, out_ref, sems):
    chunk = hbm.shape[0] // CHUNKS
    copies = []
    for c in range(CHUNKS):
        part = pl.ds(c * chunk, chunk)
        copies.append(pltpu.make_async_copy(hbm.at[part], out_ref.at[part], sems.at[c]))
        copies[-1].start()
    for copy in copies:
        copy.wait()


def stage(value):
    return pl.pallas_call(
        stage_kernel,
        out_shape=jax.ShapeDtypeStruct(value.shape, value.dtype),
        in_specs=[HBM],
        out_specs=VMEM,
        scratch_shapes=[pltpu.SemaphoreType.DMA((CHUNKS,))],
        compiler_params=pltpu.CompilerParams(vmem_limit_bytes=VMEM_BYTES),
        cost_estimate=pl.CostEstimate(flops=5*10**9, bytes_accessed=8 << 20, transcendentals=0),
        name="stage",
    )(value)


def slot_places(task_t, pos, cap):
    y, x, core = pos // (2 * SIDE), pos // 2 % SIDE, pos % 2
    owner = task_t // cap
    dy = (y - owner // (2 * SIDE)) % SIDE
    dx = (x - owner // 2 % SIDE) % SIDE
    first = jnp.where(owner % 2 == 0, dy, dx)
    second = jnp.where(owner % 2 == 0, dx, dy)
    group = jnp.where(owner % 2 == core, second, second + SIDE)
    return (group * SIDE + first) * cap + task_t % cap


def products_kernel(task_hbm, w_ref, *refs):
    parts, (out_hbm, out_ref, task_ref, t_ref, sems, out_sems) = refs[: 2 * SIDE], refs[2 * SIDE :]
    copies = [pltpu.make_async_copy(task_hbm, task_ref, sems.at[2 * SIDE])]
    count = parts[0].shape[0]
    for i, part in enumerate(parts):
        part = part.at[pl.ds(part.shape[0] - count, count)]
        copies.append(pltpu.make_async_copy(part, t_ref.at[pl.ds(i * count, count)], sems.at[i]))
    for copy in copies:
        copy.start()
    for copy in copies:
        copy.wait()
    slots, rows, cols = out_ref.shape
    per_slot = task_ref.shape[2]
    width, pieces = 4, out_sems.shape[0]
    together = slots // pieces

    def out(i):
        part = pl.ds(i * together, together)
        return pltpu.make_async_copy(out_ref.at[part], out_hbm.at[part], out_sems.at[i])

    def group(i, carry):
        for u in range(together):
            s = i * together + u
            acc = jnp.zeros((rows, cols), jnp.float32)
            for k in range(0, per_slot, width):
                left = jnp.concatenate([t_ref[task_ref[0, s, k + j]] for j in range(width)], axis=1)
                right = jnp.concatenate([w_ref[task_ref[1, s, k + j]] for j in range(width)], axis=0)
                acc = acc + jnp.dot(left, right, preferred_element_type=jnp.float32)
            out_ref[s] = acc.astype(out_ref.dtype)
        out(i).start()
        return carry

    lax.fori_loop(0, pieces, group, 0)
    for i in range(pieces):
        out(i).wait()


def products(tasks, t_parts, w_fetched):
    count, rows, cols = t_parts[0].shape
    _, slots, per_slot = tasks.shape
    return pl.pallas_call(
        products_kernel,
        out_shape=jax.ShapeDtypeStruct((slots, rows, cols), jnp.bfloat16),
        in_specs=[HBM, VMEM] + [HBM] * (2 * SIDE),
        out_specs=HBM,
        scratch_shapes=[
            pltpu.VMEM((slots, rows, cols), jnp.bfloat16),
            pltpu.SMEM(tasks.shape, tasks.dtype),
            pltpu.VMEM((2 * SIDE * count, rows, cols), jnp.bfloat16),
            pltpu.SemaphoreType.DMA((2 * SIDE + 1,)),
            pltpu.SemaphoreType.DMA((2,)),
        ],
        compiler_params=pltpu.CompilerParams(vmem_limit_bytes=VMEM_BYTES),
        cost_estimate=pl.CostEstimate(flops=2 * slots * per_slot * rows * cols * cols, bytes_accessed=7 << 20, transcendentals=0),
        name="products",
    )(tasks, w_fetched, *t_parts)


def finish_kernel(slot_ref, in_ref, inverse_ref, out_hbm, out_ref, sems):
    res_dev = out_ref.shape[0]
    chunk = res_dev // CHUNKS
    copies = []
    for c in range(CHUNKS):
        for j in range(c * chunk, (c + 1) * chunk):
            total = in_ref[slot_ref[0, j]].astype(jnp.float32) + in_ref[slot_ref[1, j]].astype(jnp.float32)
            out_ref[j] = total * inverse_ref[j]
        part = pl.ds(c * chunk, chunk)
        copies.append(pltpu.make_async_copy(out_ref.at[part], out_hbm.at[part], sems.at[c]))
        copies[-1].start()
    for copy in copies:
        copy.wait()


def finish(pair_slots, incoming, inverse):
    return pl.pallas_call(
        finish_kernel,
        out_shape=jax.ShapeDtypeStruct(inverse.shape, jnp.float32),
        in_specs=[SMEM, VMEM, VMEM],
        out_specs=HBM,
        scratch_shapes=[pltpu.VMEM(inverse.shape, jnp.float32), pltpu.SemaphoreType.DMA((CHUNKS,))],
        compiler_params=pltpu.CompilerParams(vmem_limit_bytes=VMEM_BYTES),
        name="finish",
    )(pair_slots, incoming, inverse)


def per_device(
    t2_store,
    ovvo_store,
    ovvv_store,
    dressing,
    t_home,
    t_send,
    w_home,
    w_send,
    task_t,
    task_w,
    recv_rows,
    pair_orbitals,
    eps_occ,
    eps_vir,
):
    tasks_count = lax.axis_size("tasks")
    groups = lax.axis_size("grp")
    tasks_pos = lax.axis_index("tasks")
    group_pos = lax.axis_index("grp")
    tile = t2_store.shape[2]
    slots = task_t.shape[2]
    res_dev = slots // 2

    *t_out, w_out = prepare(
        t_home, t_send[0, 0].T, t2_store[0], w_home, w_send[0].T, ovvo_store, ovvv_store, dressing
    )
    w_in = lax.all_to_all(w_out, ("tasks", "grp"), split_axis=0, concat_axis=0, tiled=True)
    t_parts, w_in = fetch_t(t_out, w_in)
    tasks = jnp.stack([slot_places(task_t[0, 0], tasks_pos, t_send.shape[3]), task_w[0, 0]])
    partials = products(tasks, t_parts, w_in)
    incoming = lax.all_to_all(partials, "tasks", split_axis=0, concat_axis=0, tiled=True)

    per_pair = NV * NV
    group_pairs = tasks_count * res_dev // per_pair
    first = tasks_pos * res_dev
    pair = pair_orbitals[group_pos * group_pairs + first // per_pair]
    occ_sum = eps_occ[pair[0]] + eps_occ[pair[1]]
    vir = eps_vir.reshape(NV, tile)
    left = lax.dynamic_slice_in_dim(vir, first // NV % NV, res_dev // NV, axis=0)
    base = occ_sum - left[:, None, :, None]
    inverse = (1.0 / (base - vir[None, :, None, :])).reshape(res_dev, tile, tile)
    named = recv_rows[0, 0].T == jnp.arange(res_dev, dtype=jnp.int32)[:, None]
    slot = jnp.arange(slots, dtype=jnp.int32)[None, :]
    low = jnp.min(jnp.where(named, slot, slots - 1), axis=1)
    high = jnp.max(jnp.where(named, slot, 0), axis=1)
    return finish(jnp.stack([low, high]), incoming, inverse)[None]


def solution(mesh):
    return jax.shard_map(
        per_device,
        mesh=mesh,
        in_specs=(
            P("grp", "tasks", None, None),
            P(("tasks", "grp"), None, None),
            P(("tasks", "grp"), None, None),
            P(),
            P("grp", None),
            P("grp", "tasks", None, None),
            P(),
            P(("tasks", "grp"), None, None),
            P("grp", "tasks", None, None),
            P("grp", "tasks", None, None),
            P("grp", "tasks", None, None),
            P(),
            P(),
            P(),
        ),
        out_specs=P("grp", "tasks", None, None),
        check_vma=False,
    )
```

```python
import jax
import jax.numpy as jnp
from jax import lax
from jax.experimental import pallas as pl
from jax.experimental.pallas import tpu as pltpu
from jax.sharding import PartitionSpec as P

NV = 8
SMEM = pl.BlockSpec(memory_space=pltpu.SMEM)
VMEM = pl.BlockSpec(memory_space=pltpu.VMEM)
HBM = pl.BlockSpec(memory_space=pltpu.HBM)
CHUNKS = 4
SIDE = 4
VMEM_MOST = 62 * 1024 * 1024
VMEM_BYTES = 16 * 1024 * 1024


def prepare_kernel(t_home_hbm, t_send_hbm, store_hbm, w_home_hbm, w_send_hbm, ovvo_hbm, ovvv_hbm, dress_hbm, *refs):
    t_outs, w_out, scratch = refs[:SIDE], refs[SIDE], refs[SIDE + 1 :]
    t_home, t_send, store, w_home, w_send, ovvo, ovvv, dress, t_stage, formed, w_stage, in_sems, t_sems, w_sems = scratch
    w_per_dev, rows, cols = formed.shape
    half = w_per_dev // 2
    pairs = [(dress_hbm, dress)]
    for c in range(2):
        part = pl.ds(c * half, half)
        pairs += [(ovvv_hbm.at[part], ovvv.at[part]), (ovvo_hbm.at[part], ovvo.at[part])]
    pairs += [(w_home_hbm, w_home), (w_send_hbm, w_send), (t_home_hbm, t_home), (t_send_hbm, t_send)]
    pairs += [(store_hbm, store)]
    loads = []
    for i, (src, dst) in enumerate(pairs):
        loads.append(pltpu.make_async_copy(src, dst, in_sems.at[i]))
        loads[-1].start()

    step = 4
    loads[0].wait()
    for c in range(2):
        loads[1 + 2 * c].wait()
        loads[2 + 2 * c].wait()
        for i in range(c * half, (c + 1) * half, step):
            block = ovvv[i : i + step].reshape(step * rows, cols)
            dressed = jnp.dot(block, dress[...], preferred_element_type=jnp.float32)
            total = ovvo[i : i + step].astype(jnp.float32) + dressed.reshape(step, rows, cols)
            formed[i : i + step] = total.astype(jnp.bfloat16)
    for load in loads[5:7]:
        load.wait()
    copies = []
    count = w_out.shape[0]
    chunk = count // CHUNKS
    for c in range(CHUNKS):

        def pick(i, carry):
            w_stage[i] = formed[lax.rem(w_home[w_send[0, i]], w_per_dev)]
            return carry

        lax.fori_loop(c * chunk, (c + 1) * chunk, pick, 0, unroll=8)
        part = pl.ds(c * chunk, chunk)
        copies.append(pltpu.make_async_copy(w_stage.at[part], w_out.at[part], w_sems.at[c]))
        copies[-1].start()

    for load in loads[7:]:
        load.wait()
    t_per_dev = store.shape[0]
    cap = t_send.shape[0]
    pos = lax.axis_index("tasks")
    y, x, core = pos // (2 * SIDE), lax.rem(pos // 2, SIDE), lax.rem(pos, 2)
    for first in (1, 2, 3, 0):
        for second in range(SIDE):
            dy = jnp.where(core == 0, first, second)
            dx = jnp.where(core == 0, second, first)
            chip = lax.rem(y + dy, SIDE) * SIDE + lax.rem(x + dx, SIDE)
            for other in range(2):
                there = chip * 2 + (1 - core if other else core)
                for c in range(cap):
                    row = lax.rem(t_home[0, t_send[c, there]], t_per_dev)
                    t_stage[first, (second * 2 + other) * cap + c] = store[row]
        copies.append(pltpu.make_async_copy(t_stage.at[first], t_outs[first], t_sems.at[first]))
        copies[-1].start()
    for copy in copies:
        copy.wait()


def prepare(t_home, t_send, store, w_home, w_send, ovvo, ovvv, dressing):
    t_count = t_send.shape[0] * t_send.shape[1]
    w_count = w_send.shape[1]
    w_per_dev, rows, cols = ovvo.shape
    t_part = jax.ShapeDtypeStruct((t_count // SIDE, rows, cols), store.dtype)
    w_all = jax.ShapeDtypeStruct((w_count, rows, cols), jnp.bfloat16)
    return pl.pallas_call(
        prepare_kernel,
        out_shape=[t_part] * SIDE + [w_all],
        in_specs=[HBM] * 8,
        out_specs=[HBM] * (SIDE + 1),
        scratch_shapes=[
            pltpu.SMEM(t_home.shape, t_home.dtype),
            pltpu.SMEM(t_send.shape, t_send.dtype),
            pltpu.VMEM(store.shape, store.dtype),
            pltpu.SMEM(w_home.shape, w_home.dtype),
            pltpu.SMEM(w_send.shape, w_send.dtype),
            pltpu.VMEM(ovvo.shape, ovvo.dtype),
            pltpu.VMEM(ovvv.shape, ovvv.dtype),
            pltpu.VMEM(dressing.shape, dressing.dtype),
            pltpu.VMEM((SIDE,) + t_part.shape, store.dtype),
            pltpu.VMEM((w_per_dev, rows, cols), jnp.bfloat16),
            pltpu.VMEM(w_all.shape, jnp.bfloat16),
            pltpu.SemaphoreType.DMA((10,)),
            pltpu.SemaphoreType.DMA((SIDE,)),
            pltpu.SemaphoreType.DMA((CHUNKS,)),
        ],
        compiler_params=pltpu.CompilerParams(vmem_limit_bytes=VMEM_MOST),
        name="prepare",
    )(t_home, t_send, store, w_home, w_send, ovvo, ovvv, dressing)


def regroup_kernel(*refs):
    ins, outs, sems = refs[:SIDE], refs[SIDE:-1], refs[-1]
    cap = ins[0].shape[0] // (2 * SIDE)
    copies = []
    for second in (2, 1, 3, 0):
        for which in (1, 0):
            for first in range(SIDE):
                src = ins[first].at[pl.ds((second * 2 + which) * cap, cap)]
                out, base = (outs[-1], (1 - which) * SIDE * cap) if second == 2 else (outs[PLACE[which, second]], 0)
                dst = out.at[pl.ds(base + first * cap, cap)]
                copies.append(pltpu.make_async_copy(src, dst, sems.at[which, second, first]))
                copies[-1].start()
    for copy in copies:
        copy.wait()


PLACE = {(0, 0): 0, (0, 1): 1, (0, 3): 2, (1, 0): 3, (1, 1): 4, (1, 3): 5}


def regroup(parts):
    count, rows, cols = parts[0].shape
    part = jax.ShapeDtypeStruct((count // 2, rows, cols), parts[0].dtype)
    return pl.pallas_call(
        regroup_kernel,
        out_shape=[part] * 6 + [jax.ShapeDtypeStruct(parts[0].shape, parts[0].dtype)],
        in_specs=[VMEM] * SIDE,
        out_specs=[HBM] * 7,
        scratch_shapes=[pltpu.SemaphoreType.DMA((2, SIDE, SIDE))],
        compiler_params=pltpu.CompilerParams(vmem_limit_bytes=VMEM_MOST),
        cost_estimate=pl.CostEstimate(flops=10**11, bytes_accessed=4 << 20, transcendentals=0),
        name="regroup",
    )(*parts)


def shift(k, first_axis):
    pairs = []
    for y in range(SIDE):
        for x in range(SIDE):
            for core in range(2):
                ty, tx = ((y + k) % SIDE, x) if core == first_axis else (y, (x + k) % SIDE)
                pairs.append(((y * SIDE + x) * 2 + core, (ty * SIDE + tx) * 2 + core))
    return pairs


def move(part, k, first_axis):
    return lax.ppermute(part, "tasks", shift(k, first_axis))


def swap_cores(part):
    return lax.ppermute(part, "tasks", [(i, i ^ 1) for i in range(2 * SIDE * SIDE)])


def fetch_t(parts, w_fetched):
    moved = {k: move(parts[k], k, 0) for k in (2, 1, 3)}
    parts = [parts[0]] + [moved[k] for k in range(1, SIDE)]
    same0, same1, same3, other0, other1, other3, both2 = regroup(parts)
    other0, other1, other3 = swap_cores(other0), swap_cores(other1), swap_cores(other3)
    same1, same3, other0, other1, other3, both2 = lax.optimization_barrier(
        (same1, same3, other0, other1, other3, both2)
    )
    both2 = move(both2, 2, 1)
    same1, other1 = move(same1, 1, 1), move(other1, 1, 0)
    same3, other3 = move(same3, 3, 1), move(other3, 3, 0)
    w_fetched, both2 = lax.optimization_barrier((stage(w_fetched), both2))
    other2 = swap_cores(both2[: both2.shape[0] // 2])
    return (same0, same1, both2, same3, other0, other1, other2, other3), w_fetched


def stage_kernel(hbm, out_ref, sems):
    chunk = hbm.shape[0] // CHUNKS
    copies = []
    for c in range(CHUNKS):
        part = pl.ds(c * chunk, chunk)
        copies.append(pltpu.make_async_copy(hbm.at[part], out_ref.at[part], sems.at[c]))
        copies[-1].start()
    for copy in copies:
        copy.wait()


def stage(value):
    return pl.pallas_call(
        stage_kernel,
        out_shape=jax.ShapeDtypeStruct(value.shape, value.dtype),
        in_specs=[HBM],
        out_specs=VMEM,
        scratch_shapes=[pltpu.SemaphoreType.DMA((CHUNKS,))],
        compiler_params=pltpu.CompilerParams(vmem_limit_bytes=VMEM_BYTES),
        cost_estimate=pl.CostEstimate(flops=5*10**9, bytes_accessed=8 << 20, transcendentals=0),
        name="stage",
    )(value)


def slot_places(task_t, pos, cap):
    y, x, core = pos // (2 * SIDE), pos // 2 % SIDE, pos % 2
    owner = task_t // cap
    dy = (y - owner // (2 * SIDE)) % SIDE
    dx = (x - owner // 2 % SIDE) % SIDE
    first = jnp.where(owner % 2 == 0, dy, dx)
    second = jnp.where(owner % 2 == 0, dx, dy)
    group = jnp.where(owner % 2 == core, second, second + SIDE)
    return (group * SIDE + first) * cap + task_t % cap


def products_kernel(task_hbm, w_ref, *refs):
    parts, (out_hbm, out_ref, task_ref, t_ref, sems, out_sems) = refs[: 2 * SIDE], refs[2 * SIDE :]
    copies = [pltpu.make_async_copy(task_hbm, task_ref, sems.at[2 * SIDE])]
    count = parts[0].shape[0]
    for i, part in enumerate(parts):
        part = part.at[pl.ds(part.shape[0] - count, count)]
        copies.append(pltpu.make_async_copy(part, t_ref.at[pl.ds(i * count, count)], sems.at[i]))
    for copy in copies:
        copy.start()
    for copy in copies:
        copy.wait()
    slots, rows, cols = out_ref.shape
    per_slot = task_ref.shape[2]
    width, pieces = 4, out_sems.shape[0]
    together = slots // pieces

    def out(i):
        part = pl.ds(i * together, together)
        return pltpu.make_async_copy(out_ref.at[part], out_hbm.at[part], out_sems.at[i])

    def group(i, carry):
        for u in range(together):
            s = i * together + u
            acc = jnp.zeros((rows, cols), jnp.float32)
            for k in range(0, per_slot, width):
                left = jnp.concatenate([t_ref[task_ref[0, s, k + j]] for j in range(width)], axis=1)
                right = jnp.concatenate([w_ref[task_ref[1, s, k + j]] for j in range(width)], axis=0)
                acc = acc + jnp.dot(left, right, preferred_element_type=jnp.float32)
            out_ref[s] = acc.astype(out_ref.dtype)
        out(i).start()
        return carry

    lax.fori_loop(0, pieces, group, 0)
    for i in range(pieces):
        out(i).wait()


def products(tasks, t_parts, w_fetched):
    count, rows, cols = t_parts[0].shape
    _, slots, per_slot = tasks.shape
    return pl.pallas_call(
        products_kernel,
        out_shape=jax.ShapeDtypeStruct((slots, rows, cols), jnp.bfloat16),
        in_specs=[HBM, VMEM] + [HBM] * (2 * SIDE),
        out_specs=HBM,
        scratch_shapes=[
            pltpu.VMEM((slots, rows, cols), jnp.bfloat16),
            pltpu.SMEM(tasks.shape, tasks.dtype),
            pltpu.VMEM((2 * SIDE * count, rows, cols), jnp.bfloat16),
            pltpu.SemaphoreType.DMA((2 * SIDE + 1,)),
            pltpu.SemaphoreType.DMA((2,)),
        ],
        compiler_params=pltpu.CompilerParams(vmem_limit_bytes=VMEM_BYTES),
        cost_estimate=pl.CostEstimate(flops=2 * slots * per_slot * rows * cols * cols, bytes_accessed=7 << 20, transcendentals=0),
        name="products",
    )(tasks, w_fetched, *t_parts)


def finish_kernel(slot_ref, in_ref, inverse_ref, out_hbm, out_ref, sems):
    res_dev = out_ref.shape[0]
    chunk = res_dev // CHUNKS
    copies = []
    for c in range(CHUNKS):
        for j in range(c * chunk, (c + 1) * chunk):
            total = in_ref[slot_ref[0, j]].astype(jnp.float32) + in_ref[slot_ref[1, j]].astype(jnp.float32)
            out_ref[j] = total * inverse_ref[j]
        part = pl.ds(c * chunk, chunk)
        copies.append(pltpu.make_async_copy(out_ref.at[part], out_hbm.at[part], sems.at[c]))
        copies[-1].start()
    for copy in copies:
        copy.wait()


def finish(pair_slots, incoming, inverse):
    return pl.pallas_call(
        finish_kernel,
        out_shape=jax.ShapeDtypeStruct(inverse.shape, jnp.float32),
        in_specs=[SMEM, VMEM, VMEM],
        out_specs=HBM,
        scratch_shapes=[pltpu.VMEM(inverse.shape, jnp.float32), pltpu.SemaphoreType.DMA((CHUNKS,))],
        compiler_params=pltpu.CompilerParams(vmem_limit_bytes=VMEM_BYTES),
        name="finish",
    )(pair_slots, incoming, inverse)


def per_device(
    t2_store,
    ovvo_store,
    ovvv_store,
    dressing,
    t_home,
    t_send,
    w_home,
    w_send,
    task_t,
    task_w,
    recv_rows,
    pair_orbitals,
    eps_occ,
    eps_vir,
):
    tasks_count = lax.axis_size("tasks")
    groups = lax.axis_size("grp")
    tasks_pos = lax.axis_index("tasks")
    group_pos = lax.axis_index("grp")
    tile = t2_store.shape[2]
    slots = task_t.shape[2]
    res_dev = slots // 2

    *t_out, w_out = prepare(
        t_home, t_send[0, 0].T, t2_store[0], w_home, w_send[0].T, ovvo_store, ovvv_store, dressing
    )
    w_in = lax.all_to_all(w_out, ("tasks", "grp"), split_axis=0, concat_axis=0, tiled=True)
    t_parts, w_in = fetch_t(t_out, w_in)
    tasks = jnp.stack([slot_places(task_t[0, 0], tasks_pos, t_send.shape[3]), task_w[0, 0]])
    partials = products(tasks, t_parts, w_in)
    incoming = lax.all_to_all(partials, "tasks", split_axis=0, concat_axis=0, tiled=True)

    per_pair = NV * NV
    group_pairs = tasks_count * res_dev // per_pair
    first = tasks_pos * res_dev
    pair = pair_orbitals[group_pos * group_pairs + first // per_pair]
    occ_sum = eps_occ[pair[0]] + eps_occ[pair[1]]
    vir = eps_vir.reshape(NV, tile)
    left = lax.dynamic_slice_in_dim(vir, first // NV % NV, res_dev // NV, axis=0)
    base = occ_sum - left[:, None, :, None]
    inverse = (1.0 / (base - vir[None, :, None, :])).reshape(res_dev, tile, tile)
    named = recv_rows[0, 0].T == jnp.arange(res_dev, dtype=jnp.int32)[:, None]
    slot = jnp.arange(slots, dtype=jnp.int32)[None, :]
    low = jnp.min(jnp.where(named, slot, slots - 1), axis=1)
    high = jnp.max(jnp.where(named, slot, 0), axis=1)
    return finish(jnp.stack([low, high]), incoming, inverse)[None]


def solution(mesh):
    return jax.shard_map(
        per_device,
        mesh=mesh,
        in_specs=(
            P("grp", "tasks", None, None),
            P(("tasks", "grp"), None, None),
            P(("tasks", "grp"), None, None),
            P(),
            P("grp", None),
            P("grp", "tasks", None, None),
            P(),
            P(("tasks", "grp"), None, None),
            P("grp", "tasks", None, None),
            P("grp", "tasks", None, None),
            P("grp", "tasks", None, None),
            P(),
            P(),
            P(),
        ),
        out_specs=P("grp", "tasks", None, None),
        check_vma=False,
    )
```
